128 devices in a mesh: grp: 2 (over core), dev: 64 (over x, y, z).
Axes of the slice: x: 4, y: 4, z: 4, core: 2. Of those that a mesh axis runs over, the one named last changes fastest.
Arguments:
- tokens: bfloat16 [8192, 4096], P('dev'), may hold values from -6 to 6
- experts: int32 [8192, 8], P('dev'), may hold values from 0 to 63, all different within a row; in each aligned block of 128 rows (0 to 127, 128 to 255, ...) at most 24 rows name the same one
- gate_weight: float32 [8192, 8], P('dev'), may hold values from 0.1 to 1
- w_gate: bfloat16 [64, 4096, 1536], P('dev', None, 'grp'), may hold values from -0.09375 to 0.09375
- w_up: bfloat16 [64, 4096, 1536], P('dev', None, 'grp'), may hold values from -0.09375 to 0.09375
- w_down: bfloat16 [64, 1536, 4096], P('dev', 'grp'), may hold values from -0.15625 to 0.15625
Outputs:
- mixed: bfloat16 [8192, 4096], P('dev')
The draws below stay inside these ranges and needn't reach their ends.
Inputs may be any that keep to these rules, and one draw needn't show every extreme that they name: In each aligned block of 128 tokens (the tokens of one index of dev) no expert is chosen more than 24 times, a bound that some block reaches; a token's 8 experts differ.
All inputs are finite; a program needn't handle non-finite values.
Results may differ from the reference program's by a relative error of at most 0.0065.
Values may be sent and summed in bfloat16 or wider, within the bound.
No kernel may reach another device: no remote copies, remote signals or barrier semaphores. Data moves between devices by JAX's collectives and lax.ppermute only.
A program may use at most 128 MiB of HBM per device.

```python
import math
import jax
import jax.numpy as jnp
import numpy as np
from jax import lax

D = 4096
FF = 1536
TOP = 8
TOK_DEV = 128
EXPERTS = 64
FFH = 768
CAP = 24
TOKENS = 8192
N_GRP = 2
N_DEV = 64


def shard_levels(stream_key, extent, cuts, low, top_value):
    def one(position, shards_of):
        draws = jax.random.uniform(jax.random.fold_in(jax.random.fold_in(stream_key, 6), position), (shards_of,), jnp.float32, low / len(cuts), top_value / len(cuts))
        return jnp.repeat(jnp.exp(draws), extent[position] // shards_of).reshape((-1,) + (1,) * (len(extent) - position - 1))

    gain = one(*cuts[0])
    for cut in cuts[1:]:
        gain = gain * one(*cut)
    return gain


def shared_out(own_key, own, number, rows, number_of, top, limit, skew):
    ranking = jax.random.permutation(own_key, number_of)
    crowded, common = portions_of(number_of, rows * top, limit, skew, True), portions_of(number_of, rows * top, limit, skew, False)
    places = jnp.arange(number_of)

    def named(tallies, rotation):
        used = int((tallies > 0).sum())
        fixed = max(1, used // 4)
        passed = fixed + (places - fixed + rotation * (used - fixed)) % max(1, number_of - fixed)
        return jnp.zeros((number_of,), jnp.int32).at[ranking[jnp.where(places < fixed, places, passed)]].set(jnp.asarray(tallies, jnp.int32))

    tallies = jnp.where(number % 4 == 0, named(crowded, number // 4), named(common, number - number // 4 - 1))
    mixed = jax.random.permutation(jax.random.fold_in(own, 3), number_of)
    donor, taker = mixed[0:number_of // 2 * 2:2], mixed[1:number_of // 2 * 2:2]
    room = jnp.minimum(tallies[donor] - 1, limit - tallies[taker]) // 2
    room = jnp.where((donor == ranking[0]) | (taker == ranking[0]) | (tallies[taker] == 0), 0, jnp.maximum(room, 0))
    passed = jax.random.randint(jax.random.fold_in(own, 4), (number_of // 2,), 0, 1 << 20) % (room + 1)
    tallies = tallies.at[donor].add(-passed).at[taker].add(passed)
    members = jnp.searchsorted(jnp.cumsum(tallies), jnp.arange(rows * top), side="right").astype(jnp.int32)
    listing = members.reshape(top, rows).T
    listing = listing[jax.random.permutation(jax.random.fold_in(own, 1), rows)]
    rotation = jax.random.randint(jax.random.fold_in(own, 2), (rows, 1), 0, top)
    return jnp.take_along_axis(listing, (jnp.arange(top)[None, :] + rotation) % top, axis=1)


def portions_of(amount, total, bound, lean, full):
    portions = [(1 << 20) // math.isqrt(grade ** lean) + 1 for grade in range(1, amount + 1)]
    largest = bound if full else min(bound, max(-(-total // amount), total * portions[0] // sum(portions)))
    least = 1 if total - largest >= amount - 1 else 0
    given, rest = [largest] + [least] * (amount - 1), total - largest - least * (amount - 1)
    while rest > 0:
        movable = [i for i in range(1, amount) if given[i] < largest] or [i for i in range(1, amount) if given[i] < bound]
        mass, remaining = sum([portions[i] for i in movable]), rest
        for i in movable:
            addition = min(bound - given[i], max(1, remaining * portions[i] // mass), rest)
            given[i] = given[i] + addition
            rest = rest - addition
    return np.array(given)


def bell_draw(key, extent, deviation, limit, cuts=(), kind=jnp.bfloat16):
    result = jax.random.normal(key, extent, jnp.float32) * deviation
    if len(cuts) > 0:
        result = shard_levels(key, extent, cuts, -0.22, 0.18) * result
    return jnp.clip(result, min=-limit, max=limit).astype(kind)


def setup_inputs(seed: int = 0) -> dict:
    streams_of = jax.random.split(jax.random.key(seed), 7)
    tokens = bell_draw(streams_of[0], (TOKENS, D), 1.0, 6.0, ((0, 64),))
    experts_keys = jax.random.split(jax.random.fold_in(streams_of[1], 1), TOKENS // TOK_DEV)
    experts_turns = jax.random.permutation(jax.random.fold_in(streams_of[1], 3), TOKENS // TOK_DEV)
    experts = jax.vmap(lambda own, number: shared_out(jax.random.fold_in(streams_of[1], 2), own, number, TOK_DEV, EXPERTS, TOP, CAP, 2))(experts_keys, experts_turns).reshape((TOKENS, TOP))
    gate_weight = jnp.clip(jnp.exp(math.log(1.0) - 2.3025851 * jax.random.uniform(streams_of[2], (TOKENS, TOP), jnp.float32) ** shard_levels(streams_of[2], (TOKENS, TOP), ((0, 64),), -0.2, 0.2)), 0.1, 1.0)
    w_gate = bell_draw(streams_of[3], (EXPERTS, D, FF), D ** -0.5, 0.09375, ((0, 64), (2, 2)))
    w_up = bell_draw(streams_of[4], (EXPERTS, D, FF), D ** -0.5, 0.09375, ((0, 64), (2, 2)))
    w_down = bell_draw(streams_of[5], (EXPERTS, FF, D), FF ** -0.5, 0.15625, ((0, 64), (1, 2)))
    return {"tokens": tokens, "experts": experts, "gate_weight": gate_weight, "w_gate": w_gate, "w_up": w_up, "w_down": w_down}


def slot_table(ids_block, n_experts):
    flat_ids = ids_block.reshape(-1)
    onehot = (flat_ids[:, None] == jnp.arange(n_experts, dtype=jnp.int32)[None, :]).astype(jnp.int32)
    ranks = jnp.cumsum(onehot, axis=0) - 1
    return jnp.sum(ranks * onehot, axis=1).astype(jnp.int32)


def reference(tokens, experts, gate_weight, w_gate, w_up, w_down):
    blocks = experts.reshape(N_DEV, TOK_DEV, TOP)
    within = jax.vmap(lambda blk: slot_table(blk, EXPERTS))(blocks)
    source = jnp.arange(N_DEV, dtype=jnp.int32)[:, None]
    flat_ids = blocks.reshape(N_DEV, TOK_DEV * TOP)
    global_slot = (flat_ids * (N_DEV * CAP) + source * CAP + within).astype(jnp.int32)
    tok_index = (source * TOK_DEV + (jnp.arange(TOK_DEV * TOP, dtype=jnp.int32) // TOP)[None, :]).astype(jnp.int32)
    total_slots = EXPERTS * N_DEV * CAP
    table = jnp.full((total_slots,), TOKENS, jnp.int32).at[global_slot.reshape(-1)].set(tok_index.reshape(-1))
    padded = jnp.concatenate([tokens, jnp.zeros((1, D), tokens.dtype)], axis=0)
    dispatched = padded[table].reshape(EXPERTS, N_DEV * CAP, D)

    def run_expert(operands):
        rows_in, gate_mat, up_mat, down_mat = operands
        total = jnp.zeros((rows_in.shape[0], D), jnp.float32)
        for half in range(N_GRP):
            start = half * FFH
            gated = jnp.dot(rows_in, gate_mat[:, start:start + FFH], preferred_element_type=jnp.float32)
            upward = jnp.dot(rows_in, up_mat[:, start:start + FFH], preferred_element_type=jnp.float32)
            act_half = (jax.nn.silu(gated) * upward).astype(jnp.bfloat16)
            part = jnp.dot(act_half, down_mat[start:start + FFH, :], preferred_element_type=jnp.float32).astype(jnp.bfloat16)
            total = total + part.astype(jnp.float32)
        return total.astype(jnp.bfloat16)

    expert_out = lax.map(run_expert, (dispatched, w_gate, w_up, w_down)).reshape(total_slots, D)
    norm = gate_weight / jnp.sum(gate_weight, axis=1, keepdims=True)

    def combine(operands):
        slots_block, norm_block = operands
        picked = expert_out[slots_block].astype(jnp.float32).reshape(TOK_DEV, TOP, D)
        return jnp.sum(picked * norm_block[:, :, None], axis=1).astype(jnp.bfloat16)

    mixed = lax.map(combine, (global_slot, norm.reshape(N_DEV, TOK_DEV, TOP)))
    return mixed.reshape(TOKENS, D)
```

```python
import jax
import jax.numpy as jnp
from jax import lax
from jax.experimental import pallas as pl
from jax.experimental.pallas import tpu as pltpu
from jax.sharding import PartitionSpec as P

LARGE, SMALL = 8, 4
SWAP = ((0, 1), (1, 0))
VMEM = 48 * 2**20
COST = pl.CostEstimate(flops=1000, bytes_accessed=1000, transcendentals=0)


def dot(a, b):
    return jnp.dot(a, b, preferred_element_type=jnp.float32)


def hidden_kernel(x, gate, up, out):
    gated = dot(x[...], gate[0])
    upward = dot(x[...], up[0])
    out[...] = (jax.nn.silu(gated) * upward).astype(out.dtype)


def hidden_units(x, w_gate, w_up):
    m, width = x.shape
    ff = w_gate.shape[2]
    block = 256
    w_spec = pl.BlockSpec((1, width, block), lambda n: (0, 0, n))
    return pl.pallas_call(
        hidden_kernel,
        out_shape=jax.ShapeDtypeStruct((m, ff), jnp.bfloat16),
        grid=(ff // block,),
        in_specs=[pl.BlockSpec((m, width), lambda n: (0, 0)), w_spec, w_spec],
        out_specs=pl.BlockSpec((m, block), lambda n: (0, n)),
        compiler_params=pltpu.CompilerParams(vmem_limit_bytes=VMEM),
        cost_estimate=COST,
        name="hidden",
    )(x, w_gate, w_up)


def down_kernel(act_a, act_b, w_a, w_b, out):
    out[...] = (dot(act_a[...], w_a[0]) + dot(act_b[...], w_b[0])).astype(out.dtype)


def down(act_a, act_b, w_a, w_b):
    m, ff = act_a.shape
    width = w_a.shape[2]
    block = 512
    act_spec = pl.BlockSpec((m, ff), lambda n: (0, 0))
    w_spec = pl.BlockSpec((1, ff, block), lambda n: (0, 0, n))
    return pl.pallas_call(
        down_kernel,
        out_shape=jax.ShapeDtypeStruct((m, width), jnp.bfloat16),
        grid=(width // block,),
        in_specs=[act_spec, act_spec, w_spec, w_spec],
        out_specs=pl.BlockSpec((m, block), lambda n: (0, n)),
        compiler_params=pltpu.CompilerParams(vmem_limit_bytes=VMEM),
        cost_estimate=COST,
        name="down",
    )(act_a, act_b, w_a, w_b)


def exchange(a):
    return lax.all_to_all(a, "dev", split_axis=0, concat_axis=0, tiled=True)


def per_device(tokens, experts, gate_weight, w_gate, w_up, w_down):
    rows, width = tokens.shape
    n = lax.axis_size("dev")
    half = width // 2
    grp = lax.axis_index("grp").astype(jnp.int32)

    hit = experts[:, :, None] == jnp.arange(n, dtype=jnp.int32)[None, None, :]
    chosen = jnp.any(hit, axis=1)
    below = jnp.tril(jnp.ones((rows, rows), jnp.bfloat16), -1)
    earlier = dot(below, chosen.astype(jnp.bfloat16))
    rank = jnp.where(chosen, earlier.astype(jnp.int32), -1)
    norm = gate_weight / jnp.sum(gate_weight, axis=1, keepdims=True)
    weight = jnp.sum(jnp.where(hit, norm[:, :, None], 0.0), axis=1)
    rank_e = rank.T

    slots_0 = LARGE * grp + jnp.arange(LARGE, dtype=jnp.int32)
    slots_1 = 2 * LARGE + SMALL * grp + jnp.arange(SMALL, dtype=jnp.int32)
    sides = jnp.arange(2, dtype=jnp.int32)
    slots_1 = jnp.broadcast_to(slots_1[None, :], (2, SMALL)).reshape(-1)
    side_1 = jnp.broadcast_to(sides[:, None], (2, SMALL)).reshape(-1)

    pick_0 = (rank_e[:, None, :] == slots_0[None, :, None]).astype(jnp.bfloat16)
    send_0 = dot(pick_0.reshape(n * LARGE, rows), tokens).astype(jnp.bfloat16)
    same_side = side_1[None, :, None, None] == sides[None, None, :, None]
    pick_1 = (
        (rank_e[:, None, None, :] == slots_1[None, :, None, None]) & same_side
    ).astype(jnp.bfloat16)
    stacked = jnp.concatenate([tokens[:, :half], tokens[:, half:]], axis=0)
    send_1 = dot(pick_1.reshape(n * 2 * SMALL, 2 * rows), stacked).astype(jnp.bfloat16)

    m_1 = n * 2 * SMALL
    at = jnp.arange(m_1, dtype=jnp.int32)
    source = (at % (m_1 // 2)) // SMALL * (2 * SMALL) + at // (m_1 // 2) * SMALL + at % SMALL
    order = (source[:, None] == at[None, :]).astype(jnp.bfloat16)

    gate_b = lax.ppermute(w_gate, "grp", SWAP)
    up_b = lax.ppermute(w_up, "grp", SWAP)
    down_b = lax.ppermute(w_down, "grp", SWAP)

    def expert(x):
        act_a = hidden_units(x, w_gate, w_up)
        act_b = hidden_units(x, gate_b, up_b)
        return down(act_a, act_b, w_down, down_b)

    x_1 = exchange(send_1.reshape(n, 2 * SMALL, half))
    x_0 = exchange(send_0.reshape(n, LARGE, width))
    x_1 = dot(order, x_1.reshape(m_1, half)).astype(jnp.bfloat16)
    done_1 = expert(jnp.concatenate([x_1[: m_1 // 2], x_1[m_1 // 2 :]], axis=1))
    done_1 = jnp.concatenate([done_1[:, :half], done_1[:, half:]], axis=0)
    done_1 = dot(order.T, done_1).astype(jnp.bfloat16).reshape(n, 2 * SMALL, half)
    x_0, done_1 = lax.optimization_barrier((x_0, done_1))
    back_1 = exchange(done_1)
    done_0 = expert(x_0.reshape(n * LARGE, width)).reshape(n, LARGE, width)
    back_1, done_0 = lax.optimization_barrier((back_1, done_0))
    back_0 = exchange(done_0)

    high = lax.reduce_precision(weight, 8, 7)
    both = jnp.stack([high, weight - high]).astype(jnp.bfloat16)
    zero = jnp.bfloat16(0)
    here = (rank[None, None, :, :, None] == slots_1) & (sides[None, :, None, None, None] == side_1)
    place_1 = jnp.where(here, both[:, None, :, :, None], zero)
    total_1 = dot(place_1.reshape(4 * rows, m_1), back_1.reshape(m_1, half))
    total_1 = (total_1[: 2 * rows] + total_1[2 * rows :]).reshape(2, rows, half)
    total_1 = jnp.concatenate([total_1[0], total_1[1]], axis=1)
    place_0 = jnp.where(
        rank[None, :, :, None] == slots_0[None, None, None, :], both[:, :, :, None], zero
    ).reshape(2 * rows, n * LARGE)
    back_0, total_1, place_0 = lax.optimization_barrier((back_0, total_1, place_0))
    total_0 = dot(place_0, back_0.reshape(n * LARGE, width))
    part = (total_0[:rows] + total_0[rows:] + total_1).astype(jnp.bfloat16)
    theirs = lax.ppermute(part, "grp", SWAP)
    return (part.astype(jnp.float32) + theirs.astype(jnp.float32)).astype(jnp.bfloat16)


def solution(mesh):
    in_specs = (
        P("dev", None),
        P("dev", None),
        P("dev", None),
        P("dev", None, "grp"),
        P("dev", None, "grp"),
        P("dev", "grp", None),
    )
    return jax.shard_map(
        per_device, mesh=mesh, in_specs=in_specs, out_specs=P("dev", None), check_vma=False
    )
```

```python
import jax
import jax.numpy as jnp
from jax import lax
from jax.experimental import pallas as pl
from jax.experimental.pallas import tpu as pltpu
from jax.sharding import PartitionSpec as P

SLOTS, QUARTERS = 6, 4
GROUP = 16
SWAP = ((0, 1), (1, 0))
VMEM = 48 * 2**20
COST = pl.CostEstimate(flops=1000, bytes_accessed=1000, transcendentals=0)


def dot(a, b):
    return jnp.dot(a, b, preferred_element_type=jnp.float32)


def order_rows(order, x, rows):
    size = order.shape[0]
    quarter = x.shape[1]
    count = size // QUARTERS
    for g in range(x.shape[0] // size):
        y = dot(order[...], x[g * size : (g + 1) * size]).astype(rows.dtype)
        for q in range(QUARTERS):
            rows[g * count : (g + 1) * count, q * quarter : (q + 1) * quarter] = y[
                q * count : (q + 1) * count
            ]


def hidden_kernel(x, gate, up, out):
    gated = dot(x[...], gate[0])
    upward = dot(x[...], up[0])
    out[...] = (jax.nn.silu(gated) * upward).astype(out.dtype)


def first_hidden_kernel(order, x, gate, up, out, rows):
    @pl.when(pl.program_id(0) == 0)
    def _():
        order_rows(order, x, rows)

    hidden_kernel(rows, gate, up, out)


def whole(shape):
    return pl.BlockSpec(shape, lambda i: (0,) * len(shape))


def params():
    return dict(
        compiler_params=pltpu.CompilerParams(vmem_limit_bytes=VMEM), cost_estimate=COST
    )


def hidden_units(x, w_gate, w_up, order=None):
    ff = w_gate.shape[2]
    width = w_gate.shape[1]
    m = x.size // width
    block = 256
    w_spec = pl.BlockSpec((1, width, block), lambda n: (0, 0, n))
    act = jax.ShapeDtypeStruct((m, ff), jnp.bfloat16)
    act_spec = pl.BlockSpec((m, block), lambda n: (0, n))
    if order is None:
        return pl.pallas_call(
            hidden_kernel,
            out_shape=act,
            grid=(ff // block,),
            in_specs=[whole(x.shape), w_spec, w_spec],
            out_specs=act_spec,
            name="hidden",
            **params(),
        )(x, w_gate, w_up)
    return pl.pallas_call(
        first_hidden_kernel,
        out_shape=[act, jax.ShapeDtypeStruct((m, width), x.dtype)],
        grid=(ff // block,),
        in_specs=[whole(order.shape), whole(x.shape), w_spec, w_spec],
        out_specs=[act_spec, whole((m, width))],
        name="first_hidden",
        **params(),
    )(order, x, w_gate, w_up)


def down_kernel(order_t, act_a, act_b, w_a, w_b, out, rows):
    step = pl.program_id(0)
    width = rows.shape[1]
    block = w_a.shape[2]
    steps = width // block
    size, quarter = out.shape
    count = size // QUARTERS

    @pl.when(step < steps)
    def _():
        part = dot(act_a[...], w_a[0]) + dot(act_b[...], w_b[0])
        rows[:, pl.ds(pl.multiple_of(step * block, block), block)] = part.astype(rows.dtype)

    @pl.when(step >= steps)
    def _():
        here = pl.ds(pl.multiple_of((step - steps) * count, count), count)
        parts = [rows[here, q * quarter : (q + 1) * quarter] for q in range(QUARTERS)]
        out[...] = dot(order_t[...], jnp.concatenate(parts, axis=0)).astype(out.dtype)


def down(order_t, act_a, act_b, w_a, w_b):
    m, ff = act_a.shape
    width = w_a.shape[2]
    block = 512
    steps = width // block
    size = order_t.shape[0]
    quarter = width // QUARTERS
    w_spec = pl.BlockSpec((1, ff, block), lambda i: (0, 0, jnp.minimum(i, steps - 1)))
    return pl.pallas_call(
        down_kernel,
        out_shape=jax.ShapeDtypeStruct((m * QUARTERS, quarter), jnp.bfloat16),
        grid=(steps + m * QUARTERS // size,),
        in_specs=[whole(order_t.shape), whole(act_a.shape), whole(act_b.shape), w_spec, w_spec],
        out_specs=pl.BlockSpec((size, quarter), lambda i: (jnp.maximum(i - steps, 0), 0)),
        scratch_shapes=[pltpu.VMEM((m, width), jnp.bfloat16)],
        name="down",
        **params(),
    )(order_t, act_a, act_b, w_a, w_b)


def pack_kernel(expand, row_slot, row_quarter, rank, tokens, out, stacked):
    quarter = out.shape[1]
    rows = tokens.shape[0]

    @pl.when(pl.program_id(0) == 0)
    def _():
        for q in range(QUARTERS):
            stacked[q * rows : (q + 1) * rows] = tokens[:, q * quarter : (q + 1) * quarter]

    found = dot(expand[...], rank[...]) == row_slot[...]
    picks = [
        jnp.where(found & (row_quarter[...] == q), 1.0, 0.0).astype(jnp.bfloat16)
        for q in range(QUARTERS)
    ]
    out[...] = dot(jnp.concatenate(picks, axis=1), stacked[...]).astype(out.dtype)


def pack(first, rank, tokens):
    n, rows = rank.shape
    quarter = tokens.shape[1] // QUARTERS
    step = 16
    part = SLOTS * QUARTERS
    at = jnp.arange(step * part, dtype=jnp.int32)
    wide = (step * part, rows)
    expand = (at[:, None] // part == jnp.arange(step)[None, :]).astype(jnp.bfloat16)
    row_slot = jnp.broadcast_to((first + at % SLOTS).astype(jnp.float32)[:, None], wide)
    row_quarter = jnp.broadcast_to((at % part // SLOTS).astype(jnp.float32)[:, None], wide)
    return pl.pallas_call(
        pack_kernel,
        out_shape=jax.ShapeDtypeStruct((n * part, quarter), jnp.bfloat16),
        grid=(n // step,),
        in_specs=[
            whole(expand.shape),
            whole(wide),
            whole(wide),
            pl.BlockSpec((step, rows), lambda i: (i, 0)),
            whole(tokens.shape),
        ],
        out_specs=pl.BlockSpec((step * part, quarter), lambda i: (i, 0)),
        scratch_shapes=[pltpu.VMEM((QUARTERS * rows, quarter), jnp.bfloat16)],
        name="pack",
        **params(),
    )(expand, row_slot, row_quarter, rank, tokens)


def combine_kernel(order, placed, back, before, out, lines):
    size, quarter = back.shape
    rows = out.shape[0]
    count = size // QUARTERS
    step = pl.program_id(0)
    y = dot(order[...], back[...]).astype(back.dtype)
    for q in range(QUARTERS):
        lines[
            pl.ds(pl.multiple_of(step * count, count), count), q * quarter : (q + 1) * quarter
        ] = y[q * count : (q + 1) * count]

    @pl.when(step == pl.num_programs(0) - 1)
    def _():
        for q in range(QUARTERS):
            here = slice(q * quarter, (q + 1) * quarter)
            both = dot(placed[...], lines[:, here])
            out[:, here] = (both[:rows] + both[rows:] + before[:, here]).astype(out.dtype)


def combine(order, placed, back, before, kind):
    size = order.shape[0]
    quarter = back.shape[1]
    return pl.pallas_call(
        combine_kernel,
        out_shape=jax.ShapeDtypeStruct(before.shape, kind),
        grid=(back.shape[0] // size,),
        in_specs=[
            whole(order.shape),
            whole(placed.shape),
            pl.BlockSpec((size, quarter), lambda i: (i, 0)),
            whole(before.shape),
        ],
        out_specs=whole(before.shape),
        scratch_shapes=[pltpu.VMEM((placed.shape[1], QUARTERS * quarter), back.dtype)],
        name="combine",
        **params(),
    )(order, placed, back, before)


def per_device(tokens, experts, gate_weight, w_gate, w_up, w_down):
    rows, width = tokens.shape
    n = lax.axis_size("dev")
    half = width // 2
    grp = lax.axis_index("grp").astype(jnp.int32)

    hit = experts[:, :, None] == jnp.arange(n, dtype=jnp.int32)[None, None, :]
    chosen = jnp.any(hit, axis=1)
    below = jnp.tril(jnp.ones((rows, rows), jnp.bfloat16), -1)
    earlier = dot(below, chosen.astype(jnp.bfloat16))
    rank = jnp.where(chosen, earlier.astype(jnp.int32), -1)
    norm = gate_weight / jnp.sum(gate_weight, axis=1, keepdims=True)
    weight = jnp.sum(jnp.where(hit, norm[:, :, None], 0.0), axis=1)
    rank_e = rank.T.astype(jnp.bfloat16)

    part = SLOTS * QUARTERS
    quarter = width // QUARTERS
    firsts = [(2 * grp + piece) * SLOTS for piece in range(2)]

    size = GROUP * part
    at = jnp.arange(size, dtype=jnp.int32)
    source = (at // SLOTS) % GROUP * part + at // (GROUP * SLOTS) * SLOTS + at % SLOTS
    order = (source[:, None] == at[None, :]).astype(jnp.bfloat16)
    order_t = (at[:, None] == source[None, :]).astype(jnp.bfloat16)

    gate_b = lax.ppermute(w_gate, "grp", SWAP)
    up_b = lax.ppermute(w_up, "grp", SWAP)
    down_b = lax.ppermute(w_down, "grp", SWAP)

    def expert(x):
        act_a, lines = hidden_units(x, w_gate, w_up, order)
        act_b = hidden_units(lines, gate_b, up_b)
        return down(order_t, act_a, act_b, w_down, down_b)

    def exchange(a):
        a = a.reshape(n, part, quarter)
        a = lax.all_to_all(a, "dev", split_axis=0, concat_axis=0, tiled=True)
        return a.reshape(n * part, quarter)

    x_0 = exchange(pack(firsts[0], rank_e, tokens))
    x_1 = exchange(pack(firsts[1], rank_e, tokens))
    done_0 = expert(x_0)
    x_1, done_0 = lax.optimization_barrier((x_1, done_0))
    back_0 = exchange(done_0)
    done_1 = expert(x_1)
    back_0, done_1 = lax.optimization_barrier((back_0, done_1))
    back_1 = exchange(done_1)

    high = lax.reduce_precision(weight, 8, 7)
    both = jnp.concatenate([high, weight - high], axis=0).astype(jnp.bfloat16)
    rank_2 = jnp.concatenate([rank, rank], axis=0)

    def place(piece):
        slots = firsts[piece] + jnp.arange(SLOTS, dtype=jnp.int32)
        at_row = jnp.where(rank_2[:, :, None] == slots, both[:, :, None], jnp.bfloat16(0))
        return at_row.reshape(2 * rows, n * SLOTS)

    nothing = jnp.zeros((rows, width), jnp.float32)
    total_0 = combine(order, place(0), back_0, nothing, jnp.float32)
    back_1, total_0, placed = lax.optimization_barrier((back_1, total_0, place(1)))
    mine = combine(order, placed, back_1, total_0, jnp.bfloat16)
    theirs = lax.ppermute(mine, "grp", SWAP)
    return (mine.astype(jnp.float32) + theirs.astype(jnp.float32)).astype(jnp.bfloat16)


def solution(mesh):
    in_specs = (
        P("dev", None),
        P("dev", None),
        P("dev", None),
        P("dev", None, "grp"),
        P("dev", None, "grp"),
        P("dev", "grp", None),
    )
    return jax.shard_map(
        per_device, mesh=mesh, in_specs=in_specs, out_specs=P("dev", None), check_vma=False
    )
```

```python
import jax
import jax.numpy as jnp
from jax import lax
from jax.experimental import pallas as pl
from jax.experimental.pallas import tpu as pltpu
from jax.sharding import PartitionSpec as P

SLOTS, QUARTERS = 6, 4
GROUP = 16
COMBINE_STEPS = 2
SWAP = ((0, 1), (1, 0))
VMEM = 48 * 2**20
COST = pl.CostEstimate(flops=1000, bytes_accessed=1000, transcendentals=0)


def dot(a, b):
    return jnp.dot(a, b, preferred_element_type=jnp.float32)


def order_rows(order, x, rows):
    size = order.shape[0]
    quarter = x.shape[1]
    count = size // QUARTERS
    for g in range(x.shape[0] // size):
        y = dot(order[...], x[g * size : (g + 1) * size]).astype(rows.dtype)
        for q in range(QUARTERS):
            rows[g * count : (g + 1) * count, q * quarter : (q + 1) * quarter] = y[
                q * count : (q + 1) * count
            ]


def hidden_kernel(x, gate, up, out):
    gated = dot(x[...], gate[0])
    upward = dot(x[...], up[0])
    out[...] = (jax.nn.silu(gated) * upward).astype(out.dtype)


def first_hidden_kernel(order, x, gate, up, out, rows):
    @pl.when(pl.program_id(0) == 0)
    def _():
        order_rows(order, x, rows)

    hidden_kernel(rows, gate, up, out)


def whole(shape):
    return pl.BlockSpec(shape, lambda i: (0,) * len(shape))


def params():
    return dict(
        compiler_params=pltpu.CompilerParams(vmem_limit_bytes=VMEM), cost_estimate=COST
    )


def hidden_units(x, w_gate, w_up, order=None):
    ff = w_gate.shape[2]
    width = w_gate.shape[1]
    m = x.size // width
    block = 256
    w_spec = pl.BlockSpec((1, width, block), lambda n: (0, 0, n))
    act = jax.ShapeDtypeStruct((m, ff), jnp.bfloat16)
    act_spec = pl.BlockSpec((m, block), lambda n: (0, n))
    if order is None:
        return pl.pallas_call(
            hidden_kernel,
            out_shape=act,
            grid=(ff // block,),
            in_specs=[whole(x.shape), w_spec, w_spec],
            out_specs=act_spec,
            name="hidden",
            **params(),
        )(x, w_gate, w_up)
    return pl.pallas_call(
        first_hidden_kernel,
        out_shape=[act, jax.ShapeDtypeStruct((m, width), x.dtype)],
        grid=(ff // block,),
        in_specs=[whole(order.shape), whole(x.shape), w_spec, w_spec],
        out_specs=[act_spec, whole((m, width))],
        name="first_hidden",
        **params(),
    )(order, x, w_gate, w_up)


def down_kernel(order_t, act_a, act_b, w_a, w_b, out, rows):
    step = pl.program_id(0)
    width = rows.shape[1]
    block = w_a.shape[2]
    steps = width // block
    size, quarter = out.shape
    count = size // QUARTERS

    @pl.when(step < steps)
    def _():
        part = dot(act_a[...], w_a[0]) + dot(act_b[...], w_b[0])
        rows[:, pl.ds(pl.multiple_of(step * block, block), block)] = part.astype(rows.dtype)

    @pl.when(step >= steps)
    def _():
        here = pl.ds(pl.multiple_of((step - steps) * count, count), count)
        parts = [rows[here, q * quarter : (q + 1) * quarter] for q in range(QUARTERS)]
        out[...] = dot(order_t[...], jnp.concatenate(parts, axis=0)).astype(out.dtype)


def down(order_t, act_a, act_b, w_a, w_b):
    m, ff = act_a.shape
    width = w_a.shape[2]
    block = 512
    steps = width // block
    size = order_t.shape[0]
    quarter = width // QUARTERS
    w_spec = pl.BlockSpec((1, ff, block), lambda i: (0, 0, jnp.minimum(i, steps - 1)))
    return pl.pallas_call(
        down_kernel,
        out_shape=jax.ShapeDtypeStruct((m * QUARTERS, quarter), jnp.bfloat16),
        grid=(steps + m * QUARTERS // size,),
        in_specs=[whole(order_t.shape), whole(act_a.shape), whole(act_b.shape), w_spec, w_spec],
        out_specs=pl.BlockSpec((size, quarter), lambda i: (jnp.maximum(i - steps, 0), 0)),
        scratch_shapes=[pltpu.VMEM((m, width), jnp.bfloat16)],
        name="down",
        **params(),
    )(order_t, act_a, act_b, w_a, w_b)


def pack_kernel(expand, row_slot, row_quarter, rank, tokens, out, stacked):
    quarter = out.shape[1]
    rows = tokens.shape[0]

    @pl.when(pl.program_id(0) == 0)
    def _():
        for q in range(QUARTERS):
            stacked[q * rows : (q + 1) * rows] = tokens[:, q * quarter : (q + 1) * quarter]

    found = dot(expand[...], rank[...]) == row_slot[...]
    picks = [
        jnp.where(found & (row_quarter[...] == q), 1.0, 0.0).astype(jnp.bfloat16)
        for q in range(QUARTERS)
    ]
    out[...] = dot(jnp.concatenate(picks, axis=1), stacked[...]).astype(out.dtype)


def pack(first, rank, tokens):
    n, rows = rank.shape
    quarter = tokens.shape[1] // QUARTERS
    step = 32
    part = SLOTS * QUARTERS
    at = jnp.arange(step * part, dtype=jnp.int32)
    wide = (step * part, rows)
    expand = (at[:, None] // part == jnp.arange(step)[None, :]).astype(jnp.bfloat16)
    row_slot = jnp.broadcast_to((first + at % SLOTS).astype(jnp.float32)[:, None], wide)
    row_quarter = jnp.broadcast_to((at % part // SLOTS).astype(jnp.float32)[:, None], wide)
    return pl.pallas_call(
        pack_kernel,
        out_shape=jax.ShapeDtypeStruct((n * part, quarter), jnp.bfloat16),
        grid=(n // step,),
        in_specs=[
            whole(expand.shape),
            whole(wide),
            whole(wide),
            pl.BlockSpec((step, rows), lambda i: (i, 0)),
            whole(tokens.shape),
        ],
        out_specs=pl.BlockSpec((step * part, quarter), lambda i: (i, 0)),
        scratch_shapes=[pltpu.VMEM((QUARTERS * rows, quarter), jnp.bfloat16)],
        name="pack",
        **params(),
    )(expand, row_slot, row_quarter, rank, tokens)


def combine_kernel(order, placed, back, before, out, lines):
    quarter = back.shape[1]
    rows = out.shape[0]
    count = back.shape[0] // QUARTERS
    step = pl.program_id(0)
    order_rows(order, back, lines.at[step])

    @pl.when(step == pl.num_programs(0) - 1)
    def _():
        for q in range(QUARTERS):
            here = slice(q * quarter, (q + 1) * quarter)
            both = before[:, here]
            for g in range(lines.shape[0]):
                product = dot(placed[:, g * count : (g + 1) * count], lines[g, :, here])
                both = both + product[:rows] + product[rows:]
            out[:, here] = both.astype(out.dtype)


def combine(order, placed, back, before, kind):
    m, quarter = back.shape
    steps = COMBINE_STEPS
    return pl.pallas_call(
        combine_kernel,
        out_shape=jax.ShapeDtypeStruct(before.shape, kind),
        grid=(steps,),
        in_specs=[
            whole(order.shape),
            whole(placed.shape),
            pl.BlockSpec((m // steps, quarter), lambda i: (i, 0)),
            whole(before.shape),
        ],
        out_specs=whole(before.shape),
        scratch_shapes=[
            pltpu.VMEM((steps, m // QUARTERS // steps, QUARTERS * quarter), back.dtype)
        ],
        name="combine",
        **params(),
    )(order, placed, back, before)


def per_device(tokens, experts, gate_weight, w_gate, w_up, w_down):
    rows, width = tokens.shape
    n = lax.axis_size("dev")
    half = width // 2
    grp = lax.axis_index("grp").astype(jnp.int32)

    hit = experts[:, :, None] == jnp.arange(n, dtype=jnp.int32)[None, None, :]
    chosen = jnp.any(hit, axis=1)
    below = jnp.tril(jnp.ones((rows, rows), jnp.bfloat16), -1)
    earlier = dot(below, chosen.astype(jnp.bfloat16))
    rank = jnp.where(chosen, earlier.astype(jnp.int32), -1)
    norm = gate_weight / jnp.sum(gate_weight, axis=1, keepdims=True)
    weight = jnp.sum(jnp.where(hit, norm[:, :, None], 0.0), axis=1)
    rank_e = rank.T.astype(jnp.bfloat16)

    part = SLOTS * QUARTERS
    quarter = width // QUARTERS
    firsts = [(2 * grp + piece) * SLOTS for piece in range(2)]

    size = GROUP * part
    at = jnp.arange(size, dtype=jnp.int32)
    source = (at // SLOTS) % GROUP * part + at // (GROUP * SLOTS) * SLOTS + at % SLOTS
    order = (source[:, None] == at[None, :]).astype(jnp.bfloat16)
    order_t = (at[:, None] == source[None, :]).astype(jnp.bfloat16)

    gate_b = lax.ppermute(w_gate, "grp", SWAP)
    up_b = lax.ppermute(w_up, "grp", SWAP)
    down_b = lax.ppermute(w_down, "grp", SWAP)

    def expert(x):
        act_a, lines = hidden_units(x, w_gate, w_up, order)
        act_b = hidden_units(lines, gate_b, up_b)
        return down(order_t, act_a, act_b, w_down, down_b)

    def exchange(a):
        a = a.reshape(n, part, quarter)
        a = lax.all_to_all(a, "dev", split_axis=0, concat_axis=0, tiled=True)
        return a.reshape(n * part, quarter)

    x_0 = exchange(pack(firsts[0], rank_e, tokens))
    x_1 = exchange(pack(firsts[1], rank_e, tokens))
    done_0 = expert(x_0)
    x_1, done_0 = lax.optimization_barrier((x_1, done_0))
    back_0 = exchange(done_0)
    done_1 = expert(x_1)
    back_0, done_1 = lax.optimization_barrier((back_0, done_1))
    back_1 = exchange(done_1)

    high = lax.reduce_precision(weight, 8, 7)
    both = jnp.concatenate([high, weight - high], axis=0).astype(jnp.bfloat16)
    rank_2 = jnp.concatenate([rank, rank], axis=0)

    def place(piece):
        slots = firsts[piece] + jnp.arange(SLOTS, dtype=jnp.int32)
        at_row = jnp.where(rank_2[:, :, None] == slots, both[:, :, None], jnp.bfloat16(0))
        return at_row.reshape(2 * rows, n * SLOTS)

    nothing = jnp.zeros((rows, width), jnp.float32)
    total_0 = combine(order, place(0), back_0, nothing, jnp.float32)
    back_1, total_0, placed = lax.optimization_barrier((back_1, total_0, place(1)))
    mine = combine(order, placed, back_1, total_0, jnp.bfloat16)
    theirs = lax.ppermute(mine, "grp", SWAP)
    return (mine.astype(jnp.float32) + theirs.astype(jnp.float32)).astype(jnp.bfloat16)


def solution(mesh):
    in_specs = (
        P("dev", None),
        P("dev", None),
        P("dev", None),
        P("dev", None, "grp"),
        P("dev", None, "grp"),
        P("dev", "grp", None),
    )
    return jax.shard_map(
        per_device, mesh=mesh, in_specs=in_specs, out_specs=P("dev", None), check_vma=False
    )
```
